1024 devices in a mesh: dp: 32 (over z), grp: 32 (over x, y, core).
Axes of the slice: x: 4, y: 4, z: 32, core: 2. Of those that a mesh axis runs over, the one named last changes fastest.
Arguments:
- acts: bfloat16 [4096, 16384], P('dp', 'grp')
- grads_out: bfloat16 [4096, 131072], P('dp', 'grp')
- owner_of: int32 [256], replicated, may hold values from 0 to 31, as said below
- factors: float32 [32, 32, 512, 512], P('grp', 'dp'), as said below
Outputs:
- new_factors: float32 [32, 32, 512, 512], P('grp', 'dp')
- preconditioned: bfloat16 [32, 32, 256, 512], P('grp', 'dp')
The draws below stay inside these ranges and needn't reach their ends.
Inputs may be any that keep to these rules, and one draw needn't show every extreme that they name: `owner_of`: the 8 blocks of one index of grp have distinct owners; each owner holds at most 16 blocks, and some owner holds exactly 16. Every factors[o, d] is symmetric positive definite.
All inputs are finite; a program needn't handle non-finite values.
Results may differ from the reference program's by a relative error of at most 0.04.
Values may be sent and summed in bfloat16 or wider, within the bound.
No kernel may reach another device: no remote copies, remote signals or barrier semaphores. Data moves between devices by JAX's collectives and lax.ppermute only.
A program may use at most 32 MiB of HBM per device.

```python
import math
import jax
import jax.numpy as jnp
from jax import lax

BLOCK = 512
TOK_DEV = 128
NEWTON = 2
BPG = 8
SLOTS = 16
NB = 256
TOKENS = 4096
IN_FEAT = 16384
OUT_FEAT = 131072
N_DP = 32
N_GRP = 32


def spread_columns(key, width_count, top_value):
    return jnp.exp(jax.random.uniform(key, (width_count,), jnp.float32, 0.0, math.log(top_value)))


def feature_values(key, row_count, width_count, overall):
    key_values, key_scale = jax.random.split(key, 2)
    values = jax.random.normal(key_values, (row_count, width_count), jnp.float32)
    scales = spread_columns(key_scale, width_count, 10.0)
    return overall * values * scales / 3.0


def draw_acts(key, part):
    key = jax.random.fold_in(key, 1)
    return feature_values(key, TOKENS, IN_FEAT, 1.0).astype(jnp.bfloat16)


def draw_grads_out(key, part):
    key = jax.random.fold_in(key, 2)
    return feature_values(key, TOKENS, OUT_FEAT, TOKENS ** (-0.5)).astype(jnp.bfloat16)


def draw_factors(key, part):
    key = jax.random.fold_in(key, 3)
    shape_all = (N_GRP, N_DP, BLOCK, BLOCK)
    base = jax.random.normal(key, shape_all, jnp.float32)
    shift_value = 0.5
    gain_value = 1.0
    product = jnp.einsum('abij,abkj->abik', base, base, precision=lax.Precision.HIGHEST) / BLOCK
    return gain_value * BLOCK * (product + shift_value * jnp.eye(BLOCK, dtype=jnp.float32))


def draw_owner_of(key, part):
    key = jax.random.fold_in(key, 4)
    key_first, key_label, key_order = jax.random.split(key, 3)
    pair_count = N_GRP // 2
    first_count = jax.random.randint(key_first, (pair_count,), 0, SLOTS + 1, dtype=jnp.int32)
    first_count = first_count.at[0].set(SLOTS)
    counts = jnp.stack([first_count, SLOTS - first_count], axis=1).reshape(N_GRP)
    labels = jax.random.permutation(key_label, N_GRP).astype(jnp.int32)
    run_order = jax.random.permutation(key_order, N_GRP)
    sequence = jnp.repeat(labels[run_order], counts[run_order], total_repeat_length=NB)
    return sequence.reshape(BPG, N_GRP).T.reshape(NB).astype(jnp.int32)


def setup_inputs(seed: int = 0) -> dict:
    seeds = jax.random.split(jax.random.key(seed), 5)
    return {
        "acts": draw_acts(jax.random.fold_in(seeds[4], 71), 0),
        "grads_out": draw_grads_out(jax.random.fold_in(seeds[4], 71), 0),
        "owner_of": draw_owner_of(jax.random.fold_in(seeds[4], 71), 0),
        "factors": draw_factors(jax.random.fold_in(seeds[4], 71), 0),
    }


decay_rate = 0.95

def inverse_root(statistic):
    highest = lax.Precision.HIGHEST
    norm_value = jnp.sqrt(jnp.sum(statistic * statistic))
    identity = jnp.eye(statistic.shape[0], dtype=jnp.float32)
    current = statistic / norm_value
    start_scale = norm_value ** (-0.25)
    estimate = identity
    for newton_step in range(NEWTON):
        factor = (5.0 * identity - current) * 0.25
        if newton_step == 0:
            estimate = start_scale * factor
        else:
            estimate = jnp.dot(estimate, factor, precision=highest)
        if newton_step + 1 < NEWTON:
            square = jnp.dot(factor, factor, precision=highest)
            fourth = jnp.dot(square, square, precision=highest)
            current = jnp.dot(fourth, current, precision=highest)
    return estimate.astype(jnp.bfloat16)

def reference(acts, grads_out, owner_of, factors):

    def block_grad(block_id):
        group_id = block_id // BPG
        inputs = lax.dynamic_slice_in_dim(acts, group_id * BLOCK, BLOCK, 1).astype(jnp.float32).reshape(N_DP, TOK_DEV, BLOCK)
        outputs = lax.dynamic_slice_in_dim(grads_out, block_id * BLOCK, BLOCK, 1).astype(jnp.float32).reshape(N_DP, TOK_DEV, BLOCK)
        partial_terms = jnp.einsum('ntr,ntc->nrc', inputs, outputs).astype(jnp.bfloat16)
        partial_terms = lax.optimization_barrier(partial_terms)
        return lax.optimization_barrier(jnp.sum(partial_terms.astype(jnp.float32), axis=0)).astype(jnp.bfloat16)
    block_ids = jnp.arange(NB, dtype=jnp.int32)
    gradient = lax.map(block_grad, block_ids)
    same_owner = owner_of[:, None] == owner_of[None, :]
    earlier = block_ids[None, :] < block_ids[:, None]
    slot_of = lax.optimization_barrier(jnp.sum((same_owner & earlier).astype(jnp.int32), axis=1)).astype(jnp.int32)
    slot_table = jnp.full((N_GRP * SLOTS,), NB, dtype=jnp.int32).at[owner_of * SLOTS + slot_of].set(block_ids)
    padded = jnp.concatenate([gradient, jnp.zeros((1, BLOCK, BLOCK), jnp.bfloat16)], axis=0)

    def one_slot(position):
        owner_id = position // SLOTS
        slot_id = position % SLOTS
        grad_block = padded[slot_table[position]]
        factor_pair = lax.dynamic_slice_in_dim(factors[owner_id], (2 * slot_id).astype(jnp.int32), 2, 0)
        left_stat = decay_rate * factor_pair[0] + jnp.dot(grad_block, grad_block.T, preferred_element_type=jnp.float32)
        right_stat = decay_rate * factor_pair[1] + jnp.dot(grad_block.T, grad_block, preferred_element_type=jnp.float32)
        left_root = inverse_root(left_stat)
        right_root = inverse_root(right_stat)
        weighted = jnp.dot(left_root, grad_block, preferred_element_type=jnp.float32).astype(jnp.bfloat16)
        update = (jnp.dot(weighted, right_root, preferred_element_type=jnp.float32) * BLOCK ** 0.5).astype(jnp.bfloat16)
        return (jnp.stack([left_stat, right_stat]), update.reshape(2, BLOCK // 2, BLOCK))
    new_stats, new_updates = lax.map(one_slot, jnp.arange(N_GRP * SLOTS, dtype=jnp.int32))
    return (new_stats.reshape(N_GRP, N_DP, BLOCK, BLOCK), new_updates.reshape(N_GRP, N_DP, BLOCK // 2, BLOCK))
```

```python
import jax
import jax.numpy as jnp
from jax import lax
from jax.experimental import pallas as pl
from jax.experimental.pallas import tpu as pltpu
from jax.sharding import PartitionSpec as P

decay_rate = 0.95
outer_gain = 1.5625
inner_gain = 2.44140625


def swapped(block):
    return lax.ppermute(
        block, "dp", [(place, place ^ 1) for place in range(lax.axis_size("dp"))]
    )


def product(left, right, contract=((1,), (0,))):
    return lax.dot_general(left, right, (contract, ((), ())), preferred_element_type=jnp.float32)


def inverse_root(statistic):
    norm_value = jnp.sqrt(jnp.sum(statistic * statistic))
    first = statistic * (0.2 / norm_value)
    first_low = first.astype(jnp.bfloat16)
    second = product(first_low, first_low)
    third = product(second.astype(jnp.bfloat16), first_low)
    tail = (-10.0 * inner_gain) * first + (5.0 * inner_gain) * second - inner_gain * third
    removed = (
        (1.0 + inner_gain) * first
        - (5.0 * inner_gain) * second
        + (10.0 * inner_gain) * third
        + product(third.astype(jnp.bfloat16), tail.astype(jnp.bfloat16))
    )
    size = statistic.shape[0]
    on_diagonal = lax.broadcasted_iota(jnp.int32, (size, size), 0) == lax.broadcasted_iota(
        jnp.int32, (size, size), 1
    )
    kept = jnp.where(on_diagonal, 1.0, 0.0) - removed
    scale = outer_gain * lax.rsqrt(jnp.sqrt(norm_value))
    return (scale * kept).astype(jnp.bfloat16)


def precondition_kernel(
    parity_ref, own_half, other_half, own_factor, other_factor, statistic_ref, update_ref,
    grad, outer, roots,
):
    parity = parity_ref[0]
    size = grad.shape[0]
    half = size // 2
    grad[:, pl.ds(pl.multiple_of(parity * half, half), half)] = own_half[...]
    grad[:, pl.ds(pl.multiple_of((1 - parity) * half, half), half)] = other_half[...]
    block = grad[...]
    outer[0] = product(block, block, ((1,), (1,)))
    outer[1] = product(block, block, ((0,), (0,)))
    statistic = decay_rate * own_factor[...] + outer[parity]
    statistic_ref[...] = statistic
    roots[parity] = inverse_root(statistic)
    partner = decay_rate * other_factor[...].astype(jnp.float32) + outer[1 - parity]
    roots[1 - parity] = inverse_root(partner)
    left_rows = roots[0, pl.ds(pl.multiple_of(parity * half, half), half), :]
    weighted = product(left_rows, block).astype(jnp.bfloat16)
    update_ref[...] = (product(weighted, roots[1]) * size**0.5).astype(jnp.bfloat16)


def precondition(parity, own_half, other_half, own_factor, other_factor):
    size = own_factor.shape[0]
    in_vmem = pl.BlockSpec(memory_space=pltpu.VMEM)
    return pl.pallas_call(
        precondition_kernel,
        out_shape=(
            jax.ShapeDtypeStruct((size, size), jnp.float32),
            jax.ShapeDtypeStruct((size // 2, size), jnp.bfloat16),
        ),
        in_specs=[pl.BlockSpec(memory_space=pltpu.SMEM)] + [in_vmem] * 4,
        out_specs=(in_vmem, in_vmem),
        scratch_shapes=[
            pltpu.VMEM((size, size), jnp.bfloat16),
            pltpu.VMEM((2, size, size), jnp.float32),
            pltpu.VMEM((2, size, size), jnp.bfloat16),
        ],
        compiler_params=pltpu.CompilerParams(vmem_limit_bytes=40 * 2**20),
        cost_estimate=pl.CostEstimate(
            flops=19 * size**3, bytes_accessed=12 * size**2, transcendentals=0
        ),
    )(parity, own_half, other_half, own_factor, other_factor)


def per_device(acts, grads_out, owner_of, factors):
    dp_count = lax.axis_size("dp")
    grp_count = lax.axis_size("grp")
    tokens, block_width = acts.shape
    half_width = block_width // 2
    per_group = grads_out.shape[1] // block_width
    pair_count = dp_count // 2
    dp_where = lax.axis_index("dp")
    grp_where = lax.axis_index("grp")
    parity = dp_where % 2
    same_parity = [[2 * pair + side for pair in range(pair_count)] for side in range(2)]

    columns = grads_out.reshape(tokens, per_group, 2, half_width)

    def side_of(side):
        taken = lax.dynamic_index_in_dim(columns, side, 2, keepdims=False)
        return taken.reshape(tokens, per_group * half_width)

    sent = jnp.concatenate([acts, side_of(1 - parity)], axis=1)
    received = swapped(sent)
    pair_acts = jnp.concatenate([acts, received[:, :block_width]], axis=0)
    pair_grads = jnp.concatenate([side_of(parity), received[:, block_width:]], axis=0)
    partial_grad = product(pair_acts, pair_grads, ((0,), (0,))).astype(jnp.bfloat16)
    summed = lax.psum_scatter(
        partial_grad, "dp", scatter_dimension=0, tiled=True, axis_index_groups=same_parity
    )
    slab_rows = block_width // pair_count
    grad_rows = summed.reshape(slab_rows, per_group, half_width)

    own_factor = factors[0, 0]
    other_factor = swapped(own_factor.astype(jnp.bfloat16))

    block_count = owner_of.shape[0]
    block_ids = jnp.arange(block_count, dtype=jnp.int32)
    same_owner = owner_of[:, None] == owner_of[None, :]
    earlier = block_ids[None, :] < block_ids[:, None]
    slot_of = jnp.sum((same_owner & earlier).astype(jnp.int32), axis=1)
    owner_ids = jnp.arange(grp_count, dtype=jnp.int32)
    local_owners = lax.dynamic_slice_in_dim(owner_of, grp_where * per_group, per_group)
    chooser = (owner_ids[:, None] == local_owners[None, :]).astype(jnp.bfloat16)
    outgoing = jnp.einsum(
        "oj,sjc->osc", chooser, grad_rows, preferred_element_type=jnp.float32
    ).astype(jnp.bfloat16)
    incoming = lax.all_to_all(outgoing, "grp", split_axis=0, concat_axis=0, tiled=True)
    held_here = owner_of == grp_where
    slot_ids = jnp.arange(pair_count, dtype=jnp.int32)
    placing = ((slot_ids[:, None] == slot_of[None, :]) & held_here[None, :]).astype(jnp.float32)
    sources = (block_ids[:, None] // per_group == owner_ids[None, :]).astype(jnp.float32)
    routing = jnp.dot(placing, sources).astype(jnp.bfloat16)
    sectioned = jnp.einsum(
        "ks,src->krc", routing, incoming, preferred_element_type=jnp.float32
    ).astype(jnp.bfloat16)
    own_half = lax.all_to_all(
        sectioned, "dp", split_axis=0, concat_axis=0, tiled=True, axis_index_groups=same_parity
    ).reshape(block_width, half_width)
    other_half = swapped(own_half)
    statistic, update = precondition(
        parity.astype(jnp.int32).reshape(1), own_half, other_half, own_factor, other_factor
    )
    return (statistic[None, None], update[None, None])


def solution(mesh):
    placed = (P("dp", "grp"), P("dp", "grp"), P(), P("grp", "dp", None, None))
    return jax.shard_map(
        per_device,
        mesh=mesh,
        in_specs=placed,
        out_specs=(P("grp", "dp", None, None), P("grp", "dp", None, None)),
        check_vma=False,
    )
```

```python
import jax
import jax.numpy as jnp
from jax import lax
from jax.experimental import pallas as pl
from jax.experimental.pallas import tpu as pltpu
from jax.sharding import PartitionSpec as P

decay_rate = 0.95
outer_gain = 1.5625
inner_gain = 2.44140625


team = 4


def across(block, mask):
    return lax.ppermute(
        block, "dp", [(place, place ^ mask) for place in range(lax.axis_size("dp"))]
    )


def along(block, distance):
    count = lax.axis_size("dp")
    return lax.ppermute(
        block, "dp", [(place, (place + distance) % count) for place in range(count)]
    )


def product(left, right, contract=((1,), (0,))):
    return lax.dot_general(left, right, (contract, ((), ())), preferred_element_type=jnp.float32)


def inverse_root(statistic):
    norm_value = jnp.sqrt(jnp.sum(statistic * statistic))
    first = statistic * (0.2 / norm_value)
    first_low = first.astype(jnp.bfloat16)
    second = product(first_low, first_low)
    third = product(second.astype(jnp.bfloat16), first_low)
    tail = (-10.0 * inner_gain) * first + (5.0 * inner_gain) * second - inner_gain * third
    removed = (
        (1.0 + inner_gain) * first
        - (5.0 * inner_gain) * second
        + (10.0 * inner_gain) * third
        + product(third.astype(jnp.bfloat16), tail.astype(jnp.bfloat16))
    )
    size = statistic.shape[0]
    on_diagonal = lax.broadcasted_iota(jnp.int32, (size, size), 0) == lax.broadcasted_iota(
        jnp.int32, (size, size), 1
    )
    kept = jnp.where(on_diagonal, 1.0, 0.0) - removed
    scale = outer_gain * lax.rsqrt(jnp.sqrt(norm_value))
    return (scale * kept).astype(jnp.bfloat16)


def precondition_kernel(
    parity_ref, own_half, other_half, own_factor, other_factor, statistic_ref, update_ref,
    grad, outer, roots,
):
    parity = parity_ref[0]
    size = grad.shape[0]
    half = size // 2
    pieces, rows, width = own_half.shape
    for piece in range(pieces):
        at = piece // 2 * rows
        for side, source in ((parity, own_half), (1 - parity, other_half)):
            grad[at : at + rows, wide(2 * side + piece % 2, width)] = source[piece]
    block = grad[...]
    outer[0] = product(block, block, ((1,), (1,)))
    outer[1] = product(block, block, ((0,), (0,)))
    statistic = decay_rate * own_factor[...] + outer[parity]
    statistic_ref[...] = statistic
    roots[parity] = inverse_root(statistic)
    partner = decay_rate * other_factor[...].astype(jnp.float32) + outer[1 - parity]
    roots[1 - parity] = inverse_root(partner)
    left_rows = roots[0, pl.ds(pl.multiple_of(parity * half, half), half), :]
    weighted = product(left_rows, block).astype(jnp.bfloat16)
    update_ref[...] = (product(weighted, roots[1]) * size**0.5).astype(jnp.bfloat16)


def precondition(parity, own_half, other_half, own_factor, other_factor):
    size = own_factor.shape[0]
    in_vmem = pl.BlockSpec(memory_space=pltpu.VMEM)
    return pl.pallas_call(
        precondition_kernel,
        out_shape=(
            jax.ShapeDtypeStruct((size, size), jnp.float32),
            jax.ShapeDtypeStruct((size // 2, size), jnp.bfloat16),
        ),
        in_specs=[pl.BlockSpec(memory_space=pltpu.SMEM)] + [in_vmem] * 4,
        out_specs=(in_vmem, in_vmem),
        scratch_shapes=[
            pltpu.VMEM((size, size), jnp.bfloat16),
            pltpu.VMEM((2, size, size), jnp.float32),
            pltpu.VMEM((2, size, size), jnp.bfloat16),
        ],
        compiler_params=pltpu.CompilerParams(vmem_limit_bytes=40 * 2**20),
        cost_estimate=pl.CostEstimate(
            flops=19 * size**3, bytes_accessed=12 * size**2, transcendentals=0
        ),
    )(parity, own_half, other_half, own_factor, other_factor)


def in_vmem():
    return pl.BlockSpec(memory_space=pltpu.VMEM)


def in_smem():
    return pl.BlockSpec(memory_space=pltpu.SMEM)


def wide(place, width):
    return pl.ds(pl.multiple_of(place * width, width), width)


def quarter_of(member):
    return 2 * (member % 2) + member // 2


def send_kernel(member_ref, acts_ref, grads_ref, *sent_refs):
    block_width = acts_ref.shape[1]
    width = block_width // team
    for mask, sent_ref in zip((2, 3, 1), sent_refs):
        quarter = quarter_of(member_ref[0] ^ mask)
        sent_ref[:, :block_width] = acts_ref[...]
        for block in range(grads_ref.shape[1] // block_width):
            at = block_width + block * width
            sent_ref[:, at : at + width] = grads_ref[:, wide(team * block + quarter, width)]


def team_messages(member, acts, grads_out):
    tokens, block_width = acts.shape
    message = jax.ShapeDtypeStruct(
        (tokens, block_width + grads_out.shape[1] // team), acts.dtype
    )
    return pl.pallas_call(
        send_kernel,
        out_shape=(message,) * 3,
        in_specs=[in_smem(), in_vmem(), in_vmem()],
        out_specs=(in_vmem(),) * 3,
        compiler_params=pltpu.CompilerParams(vmem_limit_bytes=24 * 2**20),
    )(member, acts, grads_out)


def gradient_kernel(
    member_ref, place_ref, acts_ref, grads_ref, first, second, third, partial_ref, whole
):
    block_width = acts_ref.shape[1]
    width = block_width // team
    messages = (first, second, third)
    quarter = quarter_of(member_ref[0])
    inputs = jnp.concatenate(
        [acts_ref[...]] + [message[:, :block_width] for message in messages], axis=0
    )
    blocks = grads_ref.shape[1] // block_width
    for pair in range(0, blocks, 2):
        own = jnp.concatenate(
            [grads_ref[:, wide(team * block + quarter, width)] for block in (pair, pair + 1)],
            axis=1,
        )
        at = block_width + pair * width
        cotangents = jnp.concatenate(
            [own] + [message[:, at : at + 2 * width] for message in messages], axis=0
        )
        whole[:, pair * width : (pair + 2) * width] = product(
            inputs, cotangents, ((0,), (0,))
        ).astype(whole.dtype)
    stops, rows, _ = partial_ref.shape
    for ahead in range(stops):
        stop = lax.rem(place_ref[0] + ahead, stops)
        partial_ref[ahead] = whole[wide(stop, rows), :]


def team_gradient(member, place, stops, acts, grads_out, messages):
    tokens, block_width = acts.shape
    columns = grads_out.shape[1] // team
    return pl.pallas_call(
        gradient_kernel,
        out_shape=jax.ShapeDtypeStruct((stops, block_width // stops, columns), jnp.bfloat16),
        in_specs=[in_smem()] * 2 + [in_vmem()] * 5,
        out_specs=in_vmem(),
        scratch_shapes=[pltpu.VMEM((block_width, columns), jnp.bfloat16)],
        compiler_params=pltpu.CompilerParams(vmem_limit_bytes=32 * 2**20),
        cost_estimate=pl.CostEstimate(
            flops=2 * team * tokens * block_width * columns,
            bytes_accessed=2**22,
            transcendentals=0,
        ),
    )(member, place, acts, grads_out, *messages)


def plus(left, right):
    return (left.astype(jnp.float32) + right.astype(jnp.float32)).astype(left.dtype)


def ring_terms(partial):
    stops = partial.shape[0]
    terms = [partial[0]]
    for step, length in ((1, stops // 2), (-1, stops - 1 - stops // 2)):
        if length:
            chain = partial[step * length % stops]
            for left in range(length - 1, -1, -1):
                chain = along(chain, step * team)
                if left:
                    chain = plus(chain, partial[step * left % stops])
            terms.append(chain)
    return terms


def outgoing_kernel(chosen_ref, *refs):
    *term_refs, out_ref, rows = refs
    rows[...] = sum(term[...].astype(jnp.float32) for term in term_refs).astype(rows.dtype)
    width = out_ref.shape[2]
    for owner in range(out_ref.shape[0]):
        out_ref[owner] = rows[:, wide(chosen_ref[owner], width)]


def by_owner(chosen, terms, width):
    rows, columns = terms[0].shape
    return pl.pallas_call(
        outgoing_kernel,
        out_shape=jax.ShapeDtypeStruct((chosen.shape[0], rows, width), terms[0].dtype),
        in_specs=[in_smem()] + [in_vmem()] * len(terms),
        out_specs=in_vmem(),
        scratch_shapes=[pltpu.VMEM((rows, columns), terms[0].dtype)],
        compiler_params=pltpu.CompilerParams(vmem_limit_bytes=16 * 2**20),
    )(chosen, *terms)


def slot_kernel(source_ref, incoming_ref, out_ref):
    for slot in range(out_ref.shape[0]):
        source = source_ref[slot]
        piece = incoming_ref[jnp.maximum(source, 0)]
        out_ref[slot] = jnp.where(source >= 0, piece, jnp.zeros_like(piece))


def by_slot(source, incoming):
    return pl.pallas_call(
        slot_kernel,
        out_shape=jax.ShapeDtypeStruct(
            (source.shape[0],) + incoming.shape[1:], incoming.dtype
        ),
        in_specs=[in_smem(), in_vmem()],
        out_specs=in_vmem(),
        compiler_params=pltpu.CompilerParams(vmem_limit_bytes=16 * 2**20),
    )(source, incoming)


def per_device(acts, grads_out, owner_of, factors):
    dp_count = lax.axis_size("dp")
    grp_count = lax.axis_size("grp")
    block_width = acts.shape[1]
    per_group = grads_out.shape[1] // block_width
    pair_count = dp_count // 2
    grp_where = lax.axis_index("grp")
    stops = dp_count // team
    dp_where = lax.axis_index("dp").astype(jnp.int32).reshape(1)
    parity, member, place = dp_where % 2, dp_where % team, dp_where // team
    same_parity = [[2 * pair + side for pair in range(pair_count)] for side in range(2)]

    block_count = owner_of.shape[0]
    block_ids = jnp.arange(block_count, dtype=jnp.int32)
    same_owner = owner_of[:, None] == owner_of[None, :]
    earlier = block_ids[None, :] < block_ids[:, None]
    slot_of = jnp.sum((same_owner & earlier).astype(jnp.int32), axis=1)
    owner_ids = jnp.arange(grp_count, dtype=jnp.int32)
    local_owners = lax.dynamic_slice_in_dim(owner_of, grp_where * per_group, per_group)
    local_ids = jnp.arange(per_group, dtype=jnp.int32)
    chosen = jnp.max(
        jnp.where(owner_ids[:, None] == local_owners[None, :], local_ids[None, :], 0), axis=1
    )
    slot_ids = jnp.arange(pair_count, dtype=jnp.int32)
    placing = (slot_ids[:, None] == slot_of[None, :]) & (owner_of == grp_where)[None, :]
    source = jnp.max(jnp.where(placing, block_ids[None, :] // per_group, -1), axis=1)

    sent = team_messages(member, acts, grads_out)
    messages = [across(message, mask) for mask, message in zip((2, 3, 1), sent)]
    terms = ring_terms(team_gradient(member, place, stops, acts, grads_out, messages))
    own_factor = factors[0, 0]
    outgoing, factor_low = lax.optimization_barrier(
        (by_owner(chosen, terms, block_width // team), own_factor.astype(jnp.bfloat16))
    )
    other_factor = across(factor_low, 1)
    incoming = lax.all_to_all(outgoing, "grp", split_axis=0, concat_axis=0, tiled=True)
    incoming, other_factor = lax.optimization_barrier((incoming, other_factor))
    own_half = lax.all_to_all(
        by_slot(source, incoming),
        "dp",
        split_axis=0,
        concat_axis=0,
        tiled=True,
        axis_index_groups=same_parity,
    )
    other_half = across(own_half, 1)
    statistic, update = precondition(parity, own_half, other_half, own_factor, other_factor)
    return (statistic[None, None], update[None, None])


def solution(mesh):
    placed = (P("dp", "grp"), P("dp", "grp"), P(), P("grp", "dp", None, None))
    return jax.shard_map(
        per_device,
        mesh=mesh,
        in_specs=placed,
        out_specs=(P("grp", "dp", None, None), P("grp", "dp", None, None)),
        check_vma=False,
    )
```

```python
import jax
import jax.numpy as jnp
from jax import lax
from jax.experimental import pallas as pl
from jax.experimental.pallas import tpu as pltpu
from jax.sharding import PartitionSpec as P

decay_rate = 0.95
outer_gain = 1.5625
inner_gain = 2.44140625


team = 4


def across(block, mask):
    return lax.ppermute(
        block, "dp", [(place, place ^ mask) for place in range(lax.axis_size("dp"))]
    )


def along(block, distance):
    count = lax.axis_size("dp")
    return lax.ppermute(
        block, "dp", [(place, (place + distance) % count) for place in range(count)]
    )


def product(left, right, contract=((1,), (0,))):
    return lax.dot_general(left, right, (contract, ((), ())), preferred_element_type=jnp.float32)


def inverse_root(statistic):
    norm_value = jnp.sqrt(jnp.sum(statistic * statistic))
    first = statistic * (0.2 / norm_value)
    first_low = first.astype(jnp.bfloat16)
    second = product(first_low, first_low)
    third = product(second.astype(jnp.bfloat16), first_low)
    tail = (-10.0 * inner_gain) * first + (5.0 * inner_gain) * second - inner_gain * third
    removed = (
        (1.0 + inner_gain) * first
        - (5.0 * inner_gain) * second
        + (10.0 * inner_gain) * third
        + product(third.astype(jnp.bfloat16), tail.astype(jnp.bfloat16))
    )
    size = statistic.shape[0]
    on_diagonal = lax.broadcasted_iota(jnp.int32, (size, size), 0) == lax.broadcasted_iota(
        jnp.int32, (size, size), 1
    )
    kept = jnp.where(on_diagonal, 1.0, 0.0) - removed
    scale = outer_gain * lax.rsqrt(jnp.sqrt(norm_value))
    return (scale * kept).astype(jnp.bfloat16)


def precondition_kernel(
    parity_ref, own_half, other_half, own_factor, other_factor, statistic_ref, update_ref,
    grad, outer, roots,
):
    parity = parity_ref[0]
    size = grad.shape[0]
    half = size // 2
    pieces, rows, width = own_half.shape
    for piece in range(pieces):
        at = piece // 2 * rows
        for side, source in ((parity, own_half), (1 - parity, other_half)):
            grad[at : at + rows, wide(2 * side + piece % 2, width)] = source[piece]
    block = grad[...]
    outer[0] = product(block, block, ((1,), (1,)))
    outer[1] = product(block, block, ((0,), (0,)))
    statistic = decay_rate * own_factor[...] + outer[parity]
    statistic_ref[...] = statistic
    roots[parity] = inverse_root(statistic)
    partner = decay_rate * other_factor[...].astype(jnp.float32) + outer[1 - parity]
    roots[1 - parity] = inverse_root(partner)
    left_rows = roots[0, pl.ds(pl.multiple_of(parity * half, half), half), :]
    weighted = product(left_rows, block).astype(jnp.bfloat16)
    update_ref[...] = (product(weighted, roots[1]) * size**0.5).astype(jnp.bfloat16)


def precondition(parity, own_half, other_half, own_factor, other_factor):
    size = own_factor.shape[0]
    in_vmem = pl.BlockSpec(memory_space=pltpu.VMEM)
    return pl.pallas_call(
        precondition_kernel,
        out_shape=(
            jax.ShapeDtypeStruct((size, size), jnp.float32),
            jax.ShapeDtypeStruct((size // 2, size), jnp.bfloat16),
        ),
        in_specs=[pl.BlockSpec(memory_space=pltpu.SMEM)] + [in_vmem] * 4,
        out_specs=(in_vmem, in_vmem),
        scratch_shapes=[
            pltpu.VMEM((size, size), jnp.bfloat16),
            pltpu.VMEM((2, size, size), jnp.float32),
            pltpu.VMEM((2, size, size), jnp.bfloat16),
        ],
        compiler_params=pltpu.CompilerParams(vmem_limit_bytes=40 * 2**20),
        cost_estimate=pl.CostEstimate(
            flops=19 * size**3, bytes_accessed=12 * size**2, transcendentals=0
        ),
    )(parity, own_half, other_half, own_factor, other_factor)


def in_vmem():
    return pl.BlockSpec(memory_space=pltpu.VMEM)


def in_smem():
    return pl.BlockSpec(memory_space=pltpu.SMEM)


def wide(place, width):
    return pl.ds(pl.multiple_of(place * width, width), width)


def quarter_of(member):
    return 2 * (member % 2) + member // 2


def send_kernel(member_ref, acts_ref, grads_ref, *sent_refs):
    block_width = acts_ref.shape[1]
    width = block_width // team
    for mask, sent_ref in zip((2, 3, 1), sent_refs):
        quarter = quarter_of(member_ref[0] ^ mask)
        start = 0
        if mask != 3:
            start = block_width
            sent_ref[:, :block_width] = acts_ref[...]
        for block in range(grads_ref.shape[1] // block_width):
            at = start + block * width
            sent_ref[:, at : at + width] = grads_ref[:, wide(team * block + quarter, width)]


def team_messages(member, acts, grads_out):
    tokens, block_width = acts.shape
    columns = grads_out.shape[1] // team
    return pl.pallas_call(
        send_kernel,
        out_shape=tuple(
            jax.ShapeDtypeStruct((tokens, extra + columns), acts.dtype)
            for extra in (block_width, 0, block_width)
        ),
        in_specs=[in_smem(), in_vmem(), in_vmem()],
        out_specs=(in_vmem(),) * 3,
        compiler_params=pltpu.CompilerParams(vmem_limit_bytes=24 * 2**20),
    )(member, acts, grads_out)


def gradient_kernel(
    member_ref, place_ref, acts_ref, grads_ref, first, second, third, relayed, partial_ref, whole
):
    block_width = acts_ref.shape[1]
    width = block_width // team
    quarter = quarter_of(member_ref[0])
    inputs = jnp.concatenate(
        [acts_ref[...], first[:, :block_width], relayed[...], third[:, :block_width]], axis=0
    )
    blocks = grads_ref.shape[1] // block_width
    for pair in range(0, blocks, 2):
        own = jnp.concatenate(
            [grads_ref[:, wide(team * block + quarter, width)] for block in (pair, pair + 1)],
            axis=1,
        )
        at, after = pair * width, block_width + pair * width
        cotangents = jnp.concatenate(
            [
                own,
                first[:, after : after + 2 * width],
                second[:, at : at + 2 * width],
                third[:, after : after + 2 * width],
            ],
            axis=0,
        )
        whole[:, pair * width : (pair + 2) * width] = product(
            inputs, cotangents, ((0,), (0,))
        ).astype(whole.dtype)
    stops, rows, _ = partial_ref.shape
    for ahead in range(stops):
        stop = lax.rem(place_ref[0] + ahead, stops)
        partial_ref[ahead] = whole[wide(stop, rows), :]


def team_gradient(member, place, stops, acts, grads_out, messages):
    tokens, block_width = acts.shape
    columns = grads_out.shape[1] // team
    return pl.pallas_call(
        gradient_kernel,
        out_shape=jax.ShapeDtypeStruct((stops, block_width // stops, columns), jnp.bfloat16),
        in_specs=[in_smem()] * 2 + [in_vmem()] * 6,
        out_specs=in_vmem(),
        scratch_shapes=[pltpu.VMEM((block_width, columns), jnp.bfloat16)],
        compiler_params=pltpu.CompilerParams(vmem_limit_bytes=32 * 2**20),
        cost_estimate=pl.CostEstimate(
            flops=2 * team * tokens * block_width * columns,
            bytes_accessed=2**22,
            transcendentals=0,
        ),
    )(member, place, acts, grads_out, *messages)


def plus(left, right):
    return (left.astype(jnp.float32) + right.astype(jnp.float32)).astype(left.dtype)


def ring_terms(partial):
    stops, _, columns = partial.shape
    length = stops // 2 - 1
    far = partial[length + 1]
    terms = [partial[0]]
    for step, part in ((1, slice(0, columns // 2)), (-1, slice(columns // 2, columns))):
        chain = partial[step * length % stops]
        chain = chain.at[:, part].set(plus(chain[:, part], along(far[:, part], step * team)))
        for left in range(length - 1, -1, -1):
            chain = along(chain, step * team)
            if left:
                chain = plus(chain, partial[step * left % stops])
        terms.append(chain)
    return terms


def outgoing_kernel(chosen_ref, *refs):
    *term_refs, out_ref, rows = refs
    rows[...] = sum(term[...].astype(jnp.float32) for term in term_refs).astype(rows.dtype)
    width = out_ref.shape[2]
    for owner in range(out_ref.shape[0]):
        out_ref[owner] = rows[:, wide(chosen_ref[owner], width)]


def by_owner(chosen, terms, width):
    rows, columns = terms[0].shape
    return pl.pallas_call(
        outgoing_kernel,
        out_shape=jax.ShapeDtypeStruct((chosen.shape[0], rows, width), terms[0].dtype),
        in_specs=[in_smem()] + [in_vmem()] * len(terms),
        out_specs=in_vmem(),
        scratch_shapes=[pltpu.VMEM((rows, columns), terms[0].dtype)],
        compiler_params=pltpu.CompilerParams(vmem_limit_bytes=16 * 2**20),
    )(chosen, *terms)


def slot_kernel(source_ref, incoming_ref, out_ref):
    for slot in range(out_ref.shape[0]):
        source = source_ref[slot]
        piece = incoming_ref[jnp.maximum(source, 0)]
        out_ref[slot] = jnp.where(source >= 0, piece, jnp.zeros_like(piece))


def by_slot(source, incoming):
    return pl.pallas_call(
        slot_kernel,
        out_shape=jax.ShapeDtypeStruct(
            (source.shape[0],) + incoming.shape[1:], incoming.dtype
        ),
        in_specs=[in_smem(), in_vmem()],
        out_specs=in_vmem(),
        compiler_params=pltpu.CompilerParams(vmem_limit_bytes=16 * 2**20),
    )(source, incoming)


def per_device(acts, grads_out, owner_of, factors):
    dp_count = lax.axis_size("dp")
    grp_count = lax.axis_size("grp")
    block_width = acts.shape[1]
    per_group = grads_out.shape[1] // block_width
    pair_count = dp_count // 2
    grp_where = lax.axis_index("grp")
    stops = dp_count // team
    dp_where = lax.axis_index("dp").astype(jnp.int32).reshape(1)
    parity, member, place = dp_where % 2, dp_where % team, dp_where // team
    same_parity = [[2 * pair + side for pair in range(pair_count)] for side in range(2)]

    block_count = owner_of.shape[0]
    block_ids = jnp.arange(block_count, dtype=jnp.int32)
    same_owner = owner_of[:, None] == owner_of[None, :]
    earlier = block_ids[None, :] < block_ids[:, None]
    slot_of = jnp.sum((same_owner & earlier).astype(jnp.int32), axis=1)
    owner_ids = jnp.arange(grp_count, dtype=jnp.int32)
    local_owners = lax.dynamic_slice_in_dim(owner_of, grp_where * per_group, per_group)
    local_ids = jnp.arange(per_group, dtype=jnp.int32)
    chosen = jnp.max(
        jnp.where(owner_ids[:, None] == local_owners[None, :], local_ids[None, :], 0), axis=1
    )
    slot_ids = jnp.arange(pair_count, dtype=jnp.int32)
    placing = (slot_ids[:, None] == slot_of[None, :]) & (owner_of == grp_where)[None, :]
    source = jnp.max(jnp.where(placing, block_ids[None, :] // per_group, -1), axis=1)

    own_factor = factors[0, 0]
    other_factor = across(own_factor.astype(jnp.bfloat16), 1)
    sent = team_messages(member, acts, grads_out)
    messages = [across(message, mask) for mask, message in zip((2, 3, 1), sent)]
    messages.append(across(messages[0][:, :block_width], 1))
    terms = ring_terms(team_gradient(member, place, stops, acts, grads_out, messages))
    outgoing = by_owner(chosen, terms, block_width // team)
    incoming = lax.all_to_all(outgoing, "grp", split_axis=0, concat_axis=0, tiled=True)
    incoming, other_factor = lax.optimization_barrier((incoming, other_factor))
    own_half = lax.all_to_all(
        by_slot(source, incoming),
        "dp",
        split_axis=0,
        concat_axis=0,
        tiled=True,
        axis_index_groups=same_parity,
    )
    other_half = across(own_half, 1)
    statistic, update = precondition(parity, own_half, other_half, own_factor, other_factor)
    return (statistic[None, None], update[None, None])


def solution(mesh):
    placed = (P("dp", "grp"), P("dp", "grp"), P(), P("grp", "dp", None, None))
    return jax.shard_map(
        per_device,
        mesh=mesh,
        in_specs=placed,
        out_specs=(P("grp", "dp", None, None), P("grp", "dp", None, None)),
        check_vma=False,
    )
```

```python
import jax
import jax.numpy as jnp
from jax import lax
from jax.experimental import pallas as pl
from jax.experimental.pallas import tpu as pltpu
from jax.sharding import PartitionSpec as P

decay_rate = 0.95
outer_gain = 1.5625
inner_gain = 2.44140625


team = 4


def across(block, mask):
    return lax.ppermute(
        block, "dp", [(place, place ^ mask) for place in range(lax.axis_size("dp"))]
    )


def along(block, distance):
    count = lax.axis_size("dp")
    return lax.ppermute(
        block, "dp", [(place, (place + distance) % count) for place in range(count)]
    )


def product(left, right, contract=((1,), (0,))):
    return lax.dot_general(left, right, (contract, ((), ())), preferred_element_type=jnp.float32)


def inverse_root(statistic):
    norm_value = jnp.sqrt(jnp.sum(statistic * statistic))
    first = statistic * (0.2 / norm_value)
    first_low = first.astype(jnp.bfloat16)
    second = product(first_low, first_low)
    third = product(second.astype(jnp.bfloat16), first_low)
    tail = (-10.0 * inner_gain) * first + (5.0 * inner_gain) * second - inner_gain * third
    removed = (
        (1.0 + inner_gain) * first
        - (5.0 * inner_gain) * second
        + (10.0 * inner_gain) * third
        + product(third.astype(jnp.bfloat16), tail.astype(jnp.bfloat16))
    )
    size = statistic.shape[0]
    on_diagonal = lax.broadcasted_iota(jnp.int32, (size, size), 0) == lax.broadcasted_iota(
        jnp.int32, (size, size), 1
    )
    kept = jnp.where(on_diagonal, 1.0, 0.0) - removed
    scale = outer_gain * lax.rsqrt(jnp.sqrt(norm_value))
    return (scale * kept).astype(jnp.bfloat16)


def precondition_kernel(
    parity_ref, own_half, other_half, own_factor, other_factor, statistic_ref, update_ref,
    grad, outer, roots,
):
    parity = parity_ref[0]
    size = grad.shape[0]
    half = size // 2
    pieces, rows, width = own_half.shape
    for piece in range(pieces):
        at = piece // 2 * rows
        for side, source in ((parity, own_half), (1 - parity, other_half)):
            grad[at : at + rows, wide(2 * side + piece % 2, width)] = source[piece]
    block = grad[...]
    outer[0] = product(block, block, ((1,), (1,)))
    outer[1] = product(block, block, ((0,), (0,)))
    statistic = decay_rate * own_factor[...] + outer[parity]
    statistic_ref[...] = statistic
    roots[parity] = inverse_root(statistic)
    partner = decay_rate * other_factor[...].astype(jnp.float32) + outer[1 - parity]
    roots[1 - parity] = inverse_root(partner)
    left_rows = roots[0, pl.ds(pl.multiple_of(parity * half, half), half), :]
    weighted = product(left_rows, block).astype(jnp.bfloat16)
    update_ref[...] = (product(weighted, roots[1]) * size**0.5).astype(jnp.bfloat16)


def precondition(parity, own_half, other_half, own_factor, other_factor):
    size = own_factor.shape[0]
    in_vmem = pl.BlockSpec(memory_space=pltpu.VMEM)
    return pl.pallas_call(
        precondition_kernel,
        out_shape=(
            jax.ShapeDtypeStruct((size, size), jnp.float32),
            jax.ShapeDtypeStruct((size // 2, size), jnp.bfloat16),
        ),
        in_specs=[pl.BlockSpec(memory_space=pltpu.SMEM)] + [in_vmem] * 4,
        out_specs=(in_vmem, in_vmem),
        scratch_shapes=[
            pltpu.VMEM((size, size), jnp.bfloat16),
            pltpu.VMEM((2, size, size), jnp.float32),
            pltpu.VMEM((2, size, size), jnp.bfloat16),
        ],
        compiler_params=pltpu.CompilerParams(vmem_limit_bytes=40 * 2**20),
        cost_estimate=pl.CostEstimate(
            flops=19 * size**3, bytes_accessed=12 * size**2, transcendentals=0
        ),
    )(parity, own_half, other_half, own_factor, other_factor)


def in_vmem():
    return pl.BlockSpec(memory_space=pltpu.VMEM)


def in_smem():
    return pl.BlockSpec(memory_space=pltpu.SMEM)


def wide(place, width):
    return pl.ds(pl.multiple_of(place * width, width), width)


def quarter_of(member):
    return 2 * (member % 2) + member // 2


def send_kernel(member_ref, acts_ref, grads_ref, *sent_refs):
    block_width = acts_ref.shape[1]
    width = block_width // team
    for mask, sent_ref in zip((2, 3, 1), sent_refs):
        quarter = quarter_of(member_ref[0] ^ mask)
        start = 0
        if mask != 3:
            start = block_width
            sent_ref[:, :block_width] = acts_ref[...]
        for block in range(grads_ref.shape[1] // block_width):
            at = start + block * width
            sent_ref[:, at : at + width] = grads_ref[:, wide(team * block + quarter, width)]


def team_messages(member, acts, grads_out):
    tokens, block_width = acts.shape
    columns = grads_out.shape[1] // team
    return pl.pallas_call(
        send_kernel,
        out_shape=tuple(
            jax.ShapeDtypeStruct((tokens, extra + columns), acts.dtype)
            for extra in (block_width, 0, block_width)
        ),
        in_specs=[in_smem(), in_vmem(), in_vmem()],
        out_specs=(in_vmem(),) * 3,
        compiler_params=pltpu.CompilerParams(vmem_limit_bytes=24 * 2**20),
    )(member, acts, grads_out)


def gradient_kernel(
    member_ref, place_ref, acts_ref, grads_ref, first, second, third, relayed, partial_ref, whole
):
    block_width = acts_ref.shape[1]
    width = block_width // team
    quarter = quarter_of(member_ref[0])
    inputs = jnp.concatenate(
        [acts_ref[...], first[:, :block_width], relayed[...], third[:, :block_width]], axis=0
    )
    blocks = grads_ref.shape[1] // block_width
    for pair in range(0, blocks, 2):
        own = jnp.concatenate(
            [grads_ref[:, wide(team * block + quarter, width)] for block in (pair, pair + 1)],
            axis=1,
        )
        at, after = pair * width, block_width + pair * width
        cotangents = jnp.concatenate(
            [
                own,
                first[:, after : after + 2 * width],
                second[:, at : at + 2 * width],
                third[:, after : after + 2 * width],
            ],
            axis=0,
        )
        whole[:, pair * width : (pair + 2) * width] = product(
            inputs, cotangents, ((0,), (0,))
        ).astype(whole.dtype)
    stops, rows, _ = partial_ref.shape
    for ahead in range(stops):
        stop = lax.rem(place_ref[0] + ahead, stops)
        partial_ref[ahead] = whole[wide(stop, rows), :]


def team_gradient(member, place, stops, acts, grads_out, messages):
    tokens, block_width = acts.shape
    columns = grads_out.shape[1] // team
    return pl.pallas_call(
        gradient_kernel,
        out_shape=jax.ShapeDtypeStruct((stops, block_width // stops, columns), jnp.bfloat16),
        in_specs=[in_smem()] * 2 + [in_vmem()] * 6,
        out_specs=in_vmem(),
        scratch_shapes=[pltpu.VMEM((block_width, columns), jnp.bfloat16)],
        compiler_params=pltpu.CompilerParams(vmem_limit_bytes=32 * 2**20),
        cost_estimate=pl.CostEstimate(
            flops=2 * team * tokens * block_width * columns,
            bytes_accessed=2**22,
            transcendentals=0,
        ),
    )(member, place, acts, grads_out, *messages)


def plus(left, right):
    return (left.astype(jnp.float32) + right.astype(jnp.float32)).astype(left.dtype)


def ring_terms(partial):
    stops, rows, _ = partial.shape
    length = stops // 2 - 1
    far = partial[length + 1]
    terms = [partial[0]]
    for step, part in ((1, slice(0, rows // 2)), (-1, slice(rows // 2, rows))):
        chain = partial[step * length % stops]
        chain = chain.at[part].set(plus(chain[part], along(far[part], step * team)))
        for left in range(length - 1, -1, -1):
            chain = along(chain, step * team)
            if left:
                chain = plus(chain, partial[step * left % stops])
        terms.append(chain)
    return terms


def outgoing_kernel(chosen_ref, *refs):
    *term_refs, out_ref, rows = refs
    rows[...] = sum(term[...].astype(jnp.float32) for term in term_refs).astype(rows.dtype)
    width = out_ref.shape[2]
    for owner in range(out_ref.shape[0]):
        out_ref[owner] = rows[:, wide(chosen_ref[owner], width)]


def by_owner(chosen, terms, width):
    rows, columns = terms[0].shape
    return pl.pallas_call(
        outgoing_kernel,
        out_shape=jax.ShapeDtypeStruct((chosen.shape[0], rows, width), terms[0].dtype),
        in_specs=[in_smem()] + [in_vmem()] * len(terms),
        out_specs=in_vmem(),
        scratch_shapes=[pltpu.VMEM((rows, columns), terms[0].dtype)],
        compiler_params=pltpu.CompilerParams(vmem_limit_bytes=16 * 2**20),
    )(chosen, *terms)


def slot_kernel(source_ref, incoming_ref, out_ref):
    for slot in range(out_ref.shape[0]):
        source = source_ref[slot]
        piece = incoming_ref[jnp.maximum(source, 0)]
        out_ref[slot] = jnp.where(source >= 0, piece, jnp.zeros_like(piece))


def by_slot(source, incoming):
    return pl.pallas_call(
        slot_kernel,
        out_shape=jax.ShapeDtypeStruct(
            (source.shape[0],) + incoming.shape[1:], incoming.dtype
        ),
        in_specs=[in_smem(), in_vmem()],
        out_specs=in_vmem(),
        compiler_params=pltpu.CompilerParams(vmem_limit_bytes=16 * 2**20),
    )(source, incoming)


def per_device(acts, grads_out, owner_of, factors):
    dp_count = lax.axis_size("dp")
    grp_count = lax.axis_size("grp")
    block_width = acts.shape[1]
    per_group = grads_out.shape[1] // block_width
    pair_count = dp_count // 2
    grp_where = lax.axis_index("grp")
    stops = dp_count // team
    dp_where = lax.axis_index("dp").astype(jnp.int32).reshape(1)
    parity, member, place = dp_where % 2, dp_where % team, dp_where // team
    same_parity = [[2 * pair + side for pair in range(pair_count)] for side in range(2)]

    block_count = owner_of.shape[0]
    block_ids = jnp.arange(block_count, dtype=jnp.int32)
    same_owner = owner_of[:, None] == owner_of[None, :]
    earlier = block_ids[None, :] < block_ids[:, None]
    slot_of = jnp.sum((same_owner & earlier).astype(jnp.int32), axis=1)
    owner_ids = jnp.arange(grp_count, dtype=jnp.int32)
    local_owners = lax.dynamic_slice_in_dim(owner_of, grp_where * per_group, per_group)
    local_ids = jnp.arange(per_group, dtype=jnp.int32)
    chosen = jnp.max(
        jnp.where(owner_ids[:, None] == local_owners[None, :], local_ids[None, :], 0), axis=1
    )
    slot_ids = jnp.arange(pair_count, dtype=jnp.int32)
    placing = (slot_ids[:, None] == slot_of[None, :]) & (owner_of == grp_where)[None, :]
    source = jnp.max(jnp.where(placing, block_ids[None, :] // per_group, -1), axis=1)

    own_factor = factors[0, 0]
    other_factor = across(own_factor.astype(jnp.bfloat16), 1)
    sent = team_messages(member, acts, grads_out)
    messages = [across(message, mask) for mask, message in zip((2, 3, 1), sent)]
    messages.append(across(messages[0][:, :block_width], 1))
    terms = ring_terms(team_gradient(member, place, stops, acts, grads_out, messages))
    outgoing = by_owner(chosen, terms, block_width // team)
    incoming = lax.all_to_all(outgoing, "grp", split_axis=0, concat_axis=0, tiled=True)
    incoming, other_factor = lax.optimization_barrier((incoming, other_factor))
    own_half = lax.all_to_all(
        by_slot(source, incoming),
        "dp",
        split_axis=0,
        concat_axis=0,
        tiled=True,
        axis_index_groups=same_parity,
    )
    other_half = across(own_half, 1)
    statistic, update = precondition(parity, own_half, other_half, own_factor, other_factor)
    return (statistic[None, None], update[None, None])


def solution(mesh):
    placed = (P("dp", "grp"), P("dp", "grp"), P(), P("grp", "dp", None, None))
    return jax.shard_map(
        per_device,
        mesh=mesh,
        in_specs=placed,
        out_specs=(P("grp", "dp", None, None), P("grp", "dp", None, None)),
        check_vma=False,
    )
```

```python
import jax
import jax.numpy as jnp
from jax import lax
from jax.experimental import pallas as pl
from jax.experimental.pallas import tpu as pltpu
from jax.sharding import PartitionSpec as P

decay_rate = 0.95
outer_gain = 1.5625
inner_gain = 2.44140625


team = 4


def across(block, mask):
    return lax.ppermute(
        block, "dp", [(place, place ^ mask) for place in range(lax.axis_size("dp"))]
    )


def along(block, distance):
    count = lax.axis_size("dp")
    return lax.ppermute(
        block, "dp", [(place, (place + distance) % count) for place in range(count)]
    )


def product(left, right, contract=((1,), (0,))):
    return lax.dot_general(left, right, (contract, ((), ())), preferred_element_type=jnp.float32)


def inverse_root(statistic):
    norm_value = jnp.sqrt(jnp.sum(statistic * statistic))
    first = statistic * (0.2 / norm_value)
    first_low = first.astype(jnp.bfloat16)
    second = product(first_low, first_low)
    third = product(second.astype(jnp.bfloat16), first_low)
    tail = (-10.0 * inner_gain) * first + (5.0 * inner_gain) * second - inner_gain * third
    removed = (
        (1.0 + inner_gain) * first
        - (5.0 * inner_gain) * second
        + (10.0 * inner_gain) * third
        + product(third.astype(jnp.bfloat16), tail.astype(jnp.bfloat16))
    )
    size = statistic.shape[0]
    on_diagonal = lax.broadcasted_iota(jnp.int32, (size, size), 0) == lax.broadcasted_iota(
        jnp.int32, (size, size), 1
    )
    kept = jnp.where(on_diagonal, 1.0, 0.0) - removed
    scale = outer_gain * lax.rsqrt(jnp.sqrt(norm_value))
    return (scale * kept).astype(jnp.bfloat16)


def precondition_kernel(
    parity_ref, own_half, other_half, own_factor, other_factor, statistic_ref, update_ref,
    grad, outer, roots,
):
    parity = parity_ref[0]
    size = grad.shape[0]
    half = size // 2
    pieces, rows, width = own_half.shape
    for piece in range(pieces):
        at = piece // 2 * rows
        for side, source in ((parity, own_half), (1 - parity, other_half)):
            grad[at : at + rows, wide(2 * side + piece % 2, width)] = source[piece]
    block = grad[...]
    outer[0] = product(block, block, ((1,), (1,)))
    outer[1] = product(block, block, ((0,), (0,)))
    statistic = decay_rate * own_factor[...] + outer[parity]
    statistic_ref[...] = statistic
    roots[parity] = inverse_root(statistic)
    partner = decay_rate * other_factor[...].astype(jnp.float32) + outer[1 - parity]
    roots[1 - parity] = inverse_root(partner)
    left_rows = roots[0, pl.ds(pl.multiple_of(parity * half, half), half), :]
    weighted = product(left_rows, block).astype(jnp.bfloat16)
    update_ref[...] = (product(weighted, roots[1]) * size**0.5).astype(jnp.bfloat16)


def precondition(parity, own_half, other_half, own_factor, other_factor):
    size = own_factor.shape[0]
    in_vmem = pl.BlockSpec(memory_space=pltpu.VMEM)
    return pl.pallas_call(
        precondition_kernel,
        out_shape=(
            jax.ShapeDtypeStruct((size, size), jnp.float32),
            jax.ShapeDtypeStruct((size // 2, size), jnp.bfloat16),
        ),
        in_specs=[pl.BlockSpec(memory_space=pltpu.SMEM)] + [in_vmem] * 4,
        out_specs=(in_vmem, in_vmem),
        scratch_shapes=[
            pltpu.VMEM((size, size), jnp.bfloat16),
            pltpu.VMEM((2, size, size), jnp.float32),
            pltpu.VMEM((2, size, size), jnp.bfloat16),
        ],
        compiler_params=pltpu.CompilerParams(vmem_limit_bytes=40 * 2**20),
        cost_estimate=pl.CostEstimate(
            flops=19 * size**3, bytes_accessed=12 * size**2, transcendentals=0
        ),
    )(parity, own_half, other_half, own_factor, other_factor)


def in_vmem():
    return pl.BlockSpec(memory_space=pltpu.VMEM)


def in_smem():
    return pl.BlockSpec(memory_space=pltpu.SMEM)


def wide(place, width):
    return pl.ds(pl.multiple_of(place * width, width), width)


def quarter_of(member):
    return 2 * (member % 2) + member // 2


def send_kernel(member_ref, acts_ref, grads_ref, *sent_refs):
    block_width = acts_ref.shape[1]
    width = block_width // team
    for mask, sent_ref in zip((2, 3, 1), sent_refs):
        quarter = quarter_of(member_ref[0] ^ mask)
        start = 0
        if mask != 3:
            start = block_width
            sent_ref[:, :block_width] = acts_ref[...]
        for block in range(grads_ref.shape[1] // block_width):
            at = start + block * width
            sent_ref[:, at : at + width] = grads_ref[:, wide(team * block + quarter, width)]


def team_messages(member, acts, grads_out):
    tokens, block_width = acts.shape
    columns = grads_out.shape[1] // team
    return pl.pallas_call(
        send_kernel,
        out_shape=tuple(
            jax.ShapeDtypeStruct((tokens, extra + columns), acts.dtype)
            for extra in (block_width, 0, block_width)
        ),
        in_specs=[in_smem(), in_vmem(), in_vmem()],
        out_specs=(in_vmem(),) * 3,
        compiler_params=pltpu.CompilerParams(vmem_limit_bytes=24 * 2**20),
    )(member, acts, grads_out)


def gradient_kernel(
    member_ref, place_ref, acts_ref, grads_ref, first, second, third, relayed, partial_ref, whole
):
    block_width = acts_ref.shape[1]
    width = block_width // team
    quarter = quarter_of(member_ref[0])
    inputs = jnp.concatenate(
        [acts_ref[...], first[:, :block_width], relayed[...], third[:, :block_width]], axis=0
    )
    blocks = grads_ref.shape[1] // block_width
    for pair in range(0, blocks, 2):
        own = jnp.concatenate(
            [grads_ref[:, wide(team * block + quarter, width)] for block in (pair, pair + 1)],
            axis=1,
        )
        at, after = pair * width, block_width + pair * width
        cotangents = jnp.concatenate(
            [
                own,
                first[:, after : after + 2 * width],
                second[:, at : at + 2 * width],
                third[:, after : after + 2 * width],
            ],
            axis=0,
        )
        whole[:, pair * width : (pair + 2) * width] = product(
            inputs, cotangents, ((0,), (0,))
        ).astype(whole.dtype)
    stops, rows, _ = partial_ref.shape
    for ahead in range(stops):
        stop = lax.rem(place_ref[0] + ahead, stops)
        partial_ref[ahead] = whole[wide(stop, rows), :]


def team_gradient(member, place, stops, acts, grads_out, messages):
    tokens, block_width = acts.shape
    columns = grads_out.shape[1] // team
    return pl.pallas_call(
        gradient_kernel,
        out_shape=jax.ShapeDtypeStruct((stops, block_width // stops, columns), jnp.bfloat16),
        in_specs=[in_smem()] * 2 + [in_vmem()] * 6,
        out_specs=in_vmem(),
        scratch_shapes=[pltpu.VMEM((block_width, columns), jnp.bfloat16)],
        compiler_params=pltpu.CompilerParams(vmem_limit_bytes=32 * 2**20),
        cost_estimate=pl.CostEstimate(
            flops=2 * team * tokens * block_width * columns,
            bytes_accessed=2**22,
            transcendentals=0,
        ),
    )(member, place, acts, grads_out, *messages)


def plus(left, right):
    return (left.astype(jnp.float32) + right.astype(jnp.float32)).astype(left.dtype)


def ring_terms(partial):
    stops, rows, _ = partial.shape
    length = stops // 2 - 1
    far = partial[length + 1]
    terms = [partial[0]]
    for step, part in ((1, slice(0, rows // 2)), (-1, slice(rows // 2, rows))):
        chain = partial[step * length % stops]
        chain = chain.at[part].set(plus(chain[part], along(far[part], step * team)))
        for left in range(length - 1, -1, -1):
            chain = along(chain, step * team)
            if left:
                chain = plus(chain, partial[step * left % stops])
        terms.append(chain)
    return terms


def outgoing_kernel(chosen_ref, *refs):
    *term_refs, out_ref, rows = refs
    rows[...] = sum(term[...].astype(jnp.float32) for term in term_refs).astype(rows.dtype)
    width = out_ref.shape[2]
    for owner in range(out_ref.shape[0]):
        out_ref[owner] = rows[:, wide(chosen_ref[owner], width)]


def by_owner(chosen, terms, width):
    rows, columns = terms[0].shape
    return pl.pallas_call(
        outgoing_kernel,
        out_shape=jax.ShapeDtypeStruct((chosen.shape[0], rows, width), terms[0].dtype),
        in_specs=[in_smem()] + [in_vmem()] * len(terms),
        out_specs=in_vmem(),
        scratch_shapes=[pltpu.VMEM((rows, columns), terms[0].dtype)],
        compiler_params=pltpu.CompilerParams(vmem_limit_bytes=16 * 2**20),
    )(chosen, *terms)


def slot_kernel(source_ref, incoming_ref, out_ref):
    for slot in range(out_ref.shape[0]):
        source = source_ref[slot]
        piece = incoming_ref[jnp.maximum(source, 0)]
        out_ref[slot] = jnp.where(source >= 0, piece, jnp.zeros_like(piece))


def by_slot(source, incoming):
    return pl.pallas_call(
        slot_kernel,
        out_shape=jax.ShapeDtypeStruct(
            (source.shape[0],) + incoming.shape[1:], incoming.dtype
        ),
        in_specs=[in_smem(), in_vmem()],
        out_specs=in_vmem(),
        compiler_params=pltpu.CompilerParams(vmem_limit_bytes=16 * 2**20),
    )(source, incoming)


def per_device(acts, grads_out, owner_of, factors):
    dp_count = lax.axis_size("dp")
    grp_count = lax.axis_size("grp")
    block_width = acts.shape[1]
    per_group = grads_out.shape[1] // block_width
    pair_count = dp_count // 2
    grp_where = lax.axis_index("grp")
    stops = dp_count // team
    dp_where = lax.axis_index("dp").astype(jnp.int32).reshape(1)
    parity, member, place = dp_where % 2, dp_where % team, dp_where // team
    same_parity = [[2 * pair + side for pair in range(pair_count)] for side in range(2)]

    block_count = owner_of.shape[0]
    block_ids = jnp.arange(block_count, dtype=jnp.int32)
    same_owner = owner_of[:, None] == owner_of[None, :]
    earlier = block_ids[None, :] < block_ids[:, None]
    slot_of = jnp.sum((same_owner & earlier).astype(jnp.int32), axis=1)
    owner_ids = jnp.arange(grp_count, dtype=jnp.int32)
    local_owners = lax.dynamic_slice_in_dim(owner_of, grp_where * per_group, per_group)
    local_ids = jnp.arange(per_group, dtype=jnp.int32)
    chosen = jnp.max(
        jnp.where(owner_ids[:, None] == local_owners[None, :], local_ids[None, :], 0), axis=1
    )
    slot_ids = jnp.arange(pair_count, dtype=jnp.int32)
    placing = (slot_ids[:, None] == slot_of[None, :]) & (owner_of == grp_where)[None, :]
    source = jnp.max(jnp.where(placing, block_ids[None, :] // per_group, -1), axis=1)

    own_factor = factors[0, 0]
    factor_low = own_factor.astype(jnp.bfloat16)
    sent = team_messages(member, acts, grads_out)
    messages = [across(message, mask) for mask, message in zip((2, 3, 1), sent)]
    messages.append(across(messages[0][:, :block_width], 1))
    *messages, chosen, source, factor_low = lax.optimization_barrier(
        (*messages, chosen, source, factor_low)
    )
    other_factor = across(factor_low, 1)
    terms = ring_terms(team_gradient(member, place, stops, acts, grads_out, messages))
    outgoing = by_owner(chosen, terms, block_width // team)
    incoming = lax.all_to_all(outgoing, "grp", split_axis=0, concat_axis=0, tiled=True)
    incoming, other_factor = lax.optimization_barrier((incoming, other_factor))
    own_half = lax.all_to_all(
        by_slot(source, incoming),
        "dp",
        split_axis=0,
        concat_axis=0,
        tiled=True,
        axis_index_groups=same_parity,
    )
    other_half = across(own_half, 1)
    statistic, update = precondition(parity, own_half, other_half, own_factor, other_factor)
    return (statistic[None, None], update[None, None])


def solution(mesh):
    placed = (P("dp", "grp"), P("dp", "grp"), P(), P("grp", "dp", None, None))
    return jax.shard_map(
        per_device,
        mesh=mesh,
        in_specs=placed,
        out_specs=(P("grp", "dp", None, None), P("grp", "dp", None, None)),
        check_vma=False,
    )
```
